32 devices in a mesh: fit: 2 (over x), pair: 8 (over z, y), blk: 2 (over core).
Axes of the slice: x: 2, y: 2, z: 4, core: 2. Of those that a mesh axis runs over, the one named last changes fastest.
Arguments:
- left_factor: float32 [16, 512, 2048], P('pair', 'blk', 'fit'), may hold values from -2 to 2
- right_factor: float32 [16, 512, 2048], P('pair', None, 'fit'), may hold values from -2 to 2
- amplitudes: float32 [16, 512, 512], P(('pair', 'fit'), 'blk'), may hold values from -6 to 6
- domain_trans: float32 [16, 512, 512], P(('pair', 'fit')), may hold values from -0.25 to 0.25
- vir_energy: float32 [16, 512], P(('pair', 'fit')), may hold values from 0.5 to 3
- occ_energy: float32 [16], P(('pair', 'fit')), may hold values from 0.2 to 1
- coupling: float32 [16, 4], P(('pair', 'fit')), may hold values from -4 to 4
- neighbours: int32 [16, 4], P(('pair', 'fit')), may hold values from 0 to 15, as said below
- dom_blocks: int32 [16], P(('pair', 'fit')), may hold values from 1 to 4
Outputs:
- new_amplitudes: float32 [16, 512, 512], P(('pair', 'fit'), 'blk')
- density_fit: float32 [16, 2048], P('pair', 'fit')
The draws below stay inside these ranges and needn't reach their ends.
Inputs may be any that keep to these rules, and one draw needn't show every extreme that they name: `neighbours`: with s(p) = p // 2, each entry names a pair p' with (p') % 2 equal to that of the listing pair p, and s(p') equal to s(p), s(p) + 1, s(p) - 1 or s(p) + 4, modulo 8; entries may repeat.
All inputs are finite; a program needn't handle non-finite values.
Results may differ from the reference program's by a relative error of at most 0.000068.
Values sent between devices are 32-bit elements; how exact they have to be, the bound alone decides.
A program may use at most 64 MiB of HBM per device.

```python
import math
import jax
import jax.numpy as jnp
from jax import lax

V = 512
NAUX = 2048
NB = 4
PAIR_DEV = 1
PAIRS = 16
N_FIT = 2
N_PAIR = 8


def draw_neighbours(key, part):
    total = PAIR_DEV * N_FIT * N_PAIR
    pair_ids = jnp.arange(total, dtype=jnp.int32)
    own_shard = pair_ids // (N_FIT * PAIR_DEV)
    offsets = jnp.array([0, 1, N_PAIR - 1, N_PAIR // 2], dtype=jnp.int32)
    choose = jax.random.randint(jax.random.fold_in(key, 1), (total, NB), 0, 4, dtype=jnp.int32)
    choose = choose.at[0, 0].set(0).at[total - 1, 0].set(0)
    shard = (own_shard[:, None] + offsets[choose]) % N_PAIR
    local = jax.random.randint(jax.random.fold_in(key, 3), (total, NB), 0, PAIR_DEV, dtype=jnp.int32)
    local = local.at[0, 0].set(0).at[total - 1, 0].set(PAIR_DEV - 1)
    fit_slot = pair_ids // PAIR_DEV % N_FIT
    return (shard * N_FIT + fit_slot[:, None]) * PAIR_DEV + local


def touch_ends(result, rng, low, largest):
    longest = result.shape.index(max(result.shape))
    spots = []
    for shift in (0, 1):
        where = [jax.random.randint(jax.random.fold_in(rng, axis), (), 0, length) for axis, length in enumerate(result.shape)]
        where[longest] = (where[longest] + shift) % result.shape[longest]
        spots.append(tuple(where))
    return result.at[spots[0]].set(low).at[spots[1]].set(largest)


def shard_levels(stream_key, extent, split, smallest, largest):
    gain, own = 1.0, jax.random.fold_in(stream_key, 6)
    for dim, shards_of in split:
        heights = jnp.exp(jax.random.uniform(jax.random.fold_in(own, dim), (shards_of,), jnp.float32, smallest / len(split), largest / len(split)))
        gain = gain * jnp.repeat(heights, extent[dim] // shards_of).reshape([-1 if axis == dim else 1 for axis in range(len(extent))])
    return gain


def scatter_about(stream_key, dims, scale, bound, cuts=(), kind=jnp.bfloat16):
    values = scale * jax.random.normal(stream_key, dims, jnp.float32)
    if cuts:
        values = values * shard_levels(stream_key, dims, cuts, -0.22, 0.18)
    return jnp.clip(values, -bound, bound).astype(kind)


def setup_inputs(seed: int = 0) -> dict:
    arg_keys = jax.random.split(jax.random.key(seed), 10)
    return {
        "left_factor": scatter_about(arg_keys[0], (PAIRS, V, NAUX), (NAUX ** -0.25), 2.0, ((0, 8), (1, 2), (2, 2)), jnp.float32),
        "right_factor": scatter_about(arg_keys[1], (PAIRS, V, NAUX), (NAUX ** -0.25), 2.0, ((0, 8), (2, 2)), jnp.float32),
        "amplitudes": scatter_about(arg_keys[2], (PAIRS, V, V), 0.5, 6.0, ((0, 16), (1, 2)), jnp.float32),
        "domain_trans": scatter_about(arg_keys[3], (PAIRS, V, V), V ** -0.5, 0.25, ((0, 16),), jnp.float32),
        "vir_energy": jnp.clip(jnp.exp(math.log(3.0) - 1.7917595 * jax.random.uniform(arg_keys[4], (PAIRS, V), jnp.float32) ** shard_levels(arg_keys[4], (PAIRS, V), ((0, 16),), -0.2, 0.2)), 0.5, 3.0),
        "occ_energy": jnp.clip(0.2 + 0.8 * jax.random.uniform(arg_keys[5], (PAIRS,), jnp.float32) ** shard_levels(arg_keys[5], (PAIRS,), ((0, 16),), -0.2, 0.2), 0.2, 1.0),
        "coupling": scatter_about(arg_keys[6], (PAIRS, NB), 1.0, 4.0, ((0, 16),), jnp.float32),
        "neighbours": draw_neighbours(jax.random.fold_in(arg_keys[9], 71), 0),
        "dom_blocks": touch_ends(jax.random.randint(arg_keys[8], (PAIRS,), 1, 5), jax.random.fold_in(arg_keys[8], 1), 1, 4).astype(jnp.int32),
    }


def reference(left_factor, right_factor, amplitudes, domain_trans, vir_energy, occ_energy, coupling, neighbours, dom_blocks):
    precise = lax.Precision.HIGHEST
    integrals = jnp.einsum("pad,pbd->pab", left_factor, right_factor, precision=precise)
    mixed = jnp.einsum("pab,pcb->pac", amplitudes, domain_trans, precision=precise)
    summed = jnp.zeros(amplitudes.shape, jnp.float32)
    for column in range(NB):
        summed = summed + coupling[:, column, None, None] * mixed[neighbours[:, column]]
    correction = jnp.einsum("pac,pcb->pab", summed, domain_trans, precision=precise)
    denominator = vir_energy[:, :, None] + vir_energy[:, None, :] + occ_energy[:, None, None]
    residual = integrals + denominator * amplitudes - correction
    limit = dom_blocks * (V // 4)
    position = jnp.arange(V, dtype=jnp.int32)
    inside = (position[None, :, None] < limit[:, None, None]) & (position[None, None, :] < limit[:, None, None])
    updated = amplitudes - 0.7 * residual / denominator
    new_amplitudes = jnp.where(inside, updated, jnp.zeros_like(updated))
    product = jnp.einsum("pab,pbq->paq", new_amplitudes, right_factor, precision=precise)
    density_fit = jnp.sum(left_factor * product, axis=1)
    return new_amplitudes, density_fit
```

```python
import functools

import jax
import jax.numpy as jnp
from jax import lax
from jax.experimental import pallas as pl
from jax.experimental.pallas import tpu as pltpu
from jax.sharding import PartitionSpec as P

MESH = pl.DeviceIdType.MESH
F32 = jnp.float32
BF16 = jnp.bfloat16
CHUNKS = 4
NN = (((1,), (0,)), ((), ()))
NT = (((1,), (1,)), ((), ()))


def halves(x):
    high = x.astype(BF16)
    low = (x - high.astype(F32)).astype(BF16)
    return high, low


def dot(x, y, dims):
    return lax.dot_general(x, y, dims, preferred_element_type=F32)


def dot3(x, y_high, y_low, dims):
    high, low = halves(x)
    rows = x.shape[0]
    both = dot(jnp.concatenate([high, low], axis=0), y_high, dims)
    return both[:rows] + both[rows:] + dot(high, y_low, dims)


def kernel(
    fits, pairs,
    left_hbm, right_hbm, amp_hbm, trans_hbm, vir_ref, occ_ref, coup_ref, neigh_ref, blocks_ref,
    new_hbm, dens_ref,
    left, right, amp, trans, trans_high, trans_low, right_high, right_low,
    mixed, near, part_out, part_in, own_part, base, gain, new, new_in, dens_own, dens_in,
    load_sem, mix_send, mix_recv, part_send, part_recv, new_send, new_recv, dens_send, dens_recv, out_sem,
):
    me = lax.axis_index("pair")
    fit = lax.axis_index("fit")
    blk = lax.axis_index("blk")
    rows, width = amp.shape
    size = rows // CHUNKS

    loads = [
        pltpu.make_async_copy(amp_hbm.at[0], amp, load_sem.at[0]),
        pltpu.make_async_copy(trans_hbm.at[0], trans, load_sem.at[1]),
    ]
    for j in range(fits):
        t = lax.rem(fit + j + 1, fits)
        loads.append(pltpu.make_async_copy(right_hbm.at[t], right.at[t], load_sem.at[2 + 2 * j]))
        loads.append(pltpu.make_async_copy(left_hbm.at[t], left.at[t], load_sem.at[3 + 2 * j]))
    for load in loads:
        load.start()

    steps = (1, pairs - 1, pairs // 2)
    pair_to = [{"pair": lax.rem(me + d, pairs)} for d in steps]
    fit_to = [{"fit": lax.rem(fit + j, fits)} for j in range(1, fits)]
    blk_to = {"blk": 1 - blk}
    barrier = pltpu.get_barrier_semaphore()
    targets = pair_to + fit_to + [blk_to]
    for target in targets:
        pl.semaphore_signal(barrier, inc=1, device_id=target, device_id_type=MESH)

    loads[0].wait()
    loads[1].wait()
    high, low = halves(trans[...])
    trans_high[...] = high
    trans_low[...] = low

    pl.semaphore_wait(barrier, len(targets))

    sends = []
    mix_copies = []
    for c in range(CHUNKS):
        span = pl.ds(c * size, size)
        mixed[span, :] = dot3(amp[span, :], trans_high[...], trans_low[...], NT)
        group = []
        for k in (2, 0, 1):
            copy = pltpu.make_async_remote_copy(
                src_ref=mixed.at[span],
                dst_ref=near.at[k, span],
                send_sem=mix_send.at[k, c],
                recv_sem=mix_recv.at[k, c],
                device_id=pair_to[k],
                device_id_type=MESH,
            )
            copy.start()
            group.append(copy)
        mix_copies.append(group)
        sends.extend(group)

    part_copies = []
    for j in range(fits):
        t = lax.rem(fit + j + 1, fits)
        loads[2 + 2 * j].wait()
        high, low = halves(right[t])
        right_high[t] = high
        right_low[t] = low
        loads[3 + 2 * j].wait()
        for c in range(CHUNKS):
            span = pl.ds(c * size, size)
            value = dot3(left[t, span, :], right_high[t], right_low[t], NT)
            if j == fits - 1:
                own_part[span, :] = value
                continue
            part_out[j, span, :] = value
            copy = pltpu.make_async_remote_copy(
                src_ref=part_out.at[j, span],
                dst_ref=part_in.at[j, span],
                send_sem=part_send.at[j, c],
                recv_sem=part_recv.at[j, c],
                device_id=fit_to[j],
                device_id_type=MESH,
            )
            copy.start()
            part_copies.append((c, copy))
            sends.append(copy)

    column = lax.broadcasted_iota(jnp.int32, (rows, width), 1)
    row = lax.broadcasted_iota(jnp.int32, (rows, width), 0) + blk * rows
    vir = vir_ref[...]
    vir_rows = jnp.sum(jnp.where(row == column, vir, 0.0), axis=1, keepdims=True)
    limit = blocks_ref[0] * (width // 4)
    scale = 0.7 / (vir_rows + vir + occ_ref[0])
    inside = (row < limit) & (column < limit)
    gain[...] = jnp.where(inside, scale, 0.0)
    base[...] = jnp.where(inside, 0.3 * amp[...] - scale * own_part[...], 0.0)

    weights = []
    for d in (0, pairs - 1, 1, pairs // 2):
        weight = jnp.float32(0.0)
        for k in range(coup_ref.shape[1]):
            shard = neigh_ref[0, k] // fits
            delta = lax.rem(shard - me + pairs, pairs)
            weight = weight + jnp.where(delta == d, coup_ref[0, k], 0.0)
        weights.append(weight)

    def density(f, block, span):
        product = dot3(block, right_high[f], right_low[f], NN)
        return jnp.sum(left[f, span, :] * product, axis=0, keepdims=True)

    new_copies = []
    outs = []
    dens_own[...] = jnp.zeros_like(dens_own)

    def others(c):
        span = pl.ds(c * size, size)
        for j in range(1, fits):
            new_copies[c][j - 1].wait_recv()
            f = lax.rem(fit + fits - j, fits)
            dens_own[f] += density(f, new_in[j - 1, span, :], span)

    for c in range(CHUNKS):
        span = pl.ds(c * size, size)
        for copy in mix_copies[c]:
            copy.wait_recv()
        total = weights[0] * mixed[span, :]
        for k in range(3):
            total = total + weights[k + 1] * near[k, span, :]
        value = dot3(total, trans_high[...], trans_low[...], NN)
        for step, copy in part_copies:
            if step == c:
                copy.wait_recv()
        for j in range(fits - 1):
            value = value - part_in[j, span, :]
        value = base[span, :] + gain[span, :] * value
        new[span, :] = value
        group = []
        for j in range(1, fits):
            copy = pltpu.make_async_remote_copy(
                src_ref=new.at[span],
                dst_ref=new_in.at[j - 1, span],
                send_sem=new_send.at[j - 1, c],
                recv_sem=new_recv.at[j - 1, c],
                device_id=fit_to[j - 1],
                device_id_type=MESH,
            )
            copy.start()
            group.append(copy)
            sends.append(copy)
        new_copies.append(group)
        out = pltpu.make_async_copy(new.at[span], new_hbm.at[0, span], out_sem.at[c])
        out.start()
        outs.append(out)
        dens_own[fit] += density(fit, new[span, :], span)
        if c > 0:
            others(c - 1)
    others(CHUNKS - 1)

    copy = pltpu.make_async_remote_copy(
        src_ref=dens_own, dst_ref=dens_in, send_sem=dens_send, recv_sem=dens_recv,
        device_id=blk_to, device_id_type=MESH,
    )
    copy.start()
    for send in sends:
        send.wait_send()
    for out in outs:
        out.wait()
    copy.wait()
    for f in range(fits):
        dens_ref[f : f + 1, :] = dens_own[f] + dens_in[f]


def body(fits, pairs, left, right, amp, trans, vir, occ, coup, neigh, blocks):
    rows, width = amp.shape[1:]
    aux = left.shape[2]
    hbm = pl.BlockSpec(memory_space=pl.ANY)
    vmem = pl.BlockSpec(memory_space=pltpu.VMEM)
    smem = pl.BlockSpec(memory_space=pltpu.SMEM)
    dma = pltpu.SemaphoreType.DMA
    plane = pltpu.VMEM((rows, width), F32)
    flops = 2 * 3 * 2 * (fits * rows * width * aux + rows * width * width)
    return pl.pallas_call(
        functools.partial(kernel, fits, pairs),
        out_shape=(
            jax.ShapeDtypeStruct(amp.shape, F32),
            jax.ShapeDtypeStruct((fits, aux), F32),
        ),
        in_specs=[hbm] * 4 + [vmem] + [smem] * 4,
        out_specs=(hbm, vmem),
        scratch_shapes=[
            pltpu.VMEM((fits, rows, aux), F32),
            pltpu.VMEM((fits, width, aux), F32),
            plane,
            pltpu.VMEM((width, width), F32),
            pltpu.VMEM((width, width), BF16),
            pltpu.VMEM((width, width), BF16),
            pltpu.VMEM((fits, width, aux), BF16),
            pltpu.VMEM((fits, width, aux), BF16),
            plane,
            pltpu.VMEM((3, rows, width), F32),
            pltpu.VMEM((fits - 1, rows, width), F32),
            pltpu.VMEM((fits - 1, rows, width), F32),
            plane,
            plane,
            plane,
            plane,
            pltpu.VMEM((fits - 1, rows, width), F32),
            pltpu.VMEM((fits, 1, aux), F32),
            pltpu.VMEM((fits, 1, aux), F32),
            dma((2 + 2 * fits,)),
            dma((3, CHUNKS)),
            dma((3, CHUNKS)),
            dma((fits - 1, CHUNKS)),
            dma((fits - 1, CHUNKS)),
            dma((fits - 1, CHUNKS)),
            dma((fits - 1, CHUNKS)),
            dma,
            dma,
            dma((CHUNKS,)),
        ],
        compiler_params=pltpu.CompilerParams(
            collective_id=0, has_side_effects=True, vmem_limit_bytes=48 * 2**20
        ),
        cost_estimate=pl.CostEstimate(flops=flops, bytes_accessed=2**23, transcendentals=0),
    )(left, right, amp, trans, vir, occ, coup, neigh, blocks)


def solution(mesh):
    placed = (
        P("pair", "blk", "fit"),
        P("pair", None, "fit"),
        P(("pair", "fit"), "blk", None),
        P(("pair", "fit"), None, None),
        P(("pair", "fit"), None),
        P(("pair", "fit")),
        P(("pair", "fit"), None),
        P(("pair", "fit"), None),
        P(("pair", "fit")),
    )
    return jax.shard_map(
        functools.partial(body, mesh.shape["fit"], mesh.shape["pair"]),
        mesh=mesh,
        in_specs=placed,
        out_specs=(P(("pair", "fit"), "blk", None), P("pair", "fit")),
        check_vma=False,
    )
```

```python
import functools

import jax
import jax.numpy as jnp
from jax import lax
from jax.experimental import pallas as pl
from jax.experimental.pallas import tpu as pltpu
from jax.sharding import PartitionSpec as P

MESH = pl.DeviceIdType.MESH
F32 = jnp.float32
BF16 = jnp.bfloat16
CHUNKS = 4
PARTS = 2
GROUPS = (2, 1, 1)
WINDOW = 1
AHEAD = 1
OWN = 3
NN = (((1,), (0,)), ((), ()))
NT = (((1,), (1,)), ((), ()))


def halves(x):
    high = x.astype(BF16)
    low = (x - high.astype(F32)).astype(BF16)
    return high, low


def dot(x, y, dims):
    return lax.dot_general(x, y, dims, preferred_element_type=F32)


def dot3(x, y_high, y_low, dims):
    high, low = halves(x)
    rows = x.shape[0]
    both = dot(jnp.concatenate([high, low], axis=0), y_high, dims)
    return both[:rows] + both[rows:] + dot(high, y_low, dims)


def kernel(
    fits, pairs,
    left_hbm, right_hbm, amp_hbm, trans_hbm, vir_hbm, occ_hbm, coup_hbm, neigh_hbm, blocks_hbm,
    new_hbm, dens_ref,
    left, right, amp, trans, vir_ref, occ_ref, coup_ref, neigh_ref, blocks_ref,
    trans_high, trans_low, right_high, right_low,
    held, part_out, part_in, own_part, base, gain, new, new_in, dens_own, dens_in,
    load_sem, mix_send, mix_recv, part_send, part_recv, new_send, new_recv, dens_send, dens_recv, out_sem,
):
    me = lax.axis_index("pair")
    fit = lax.axis_index("fit")
    blk = lax.axis_index("blk")
    rows, width = amp.shape
    size = rows // CHUNKS
    part_size = rows // PARTS

    pieces = [
        (amp_hbm.at[0], amp), (trans_hbm.at[0], trans), (vir_hbm, vir_ref), (occ_hbm, occ_ref),
        (coup_hbm, coup_ref), (neigh_hbm, neigh_ref), (blocks_hbm, blocks_ref),
    ]
    small = len(pieces)
    for j in range(fits):
        t = lax.rem(fit + j + 1, fits)
        pieces += [(right_hbm.at[t], right.at[t]), (left_hbm.at[t], left.at[t])]
    loads = [pltpu.make_async_copy(src, dst, load_sem.at[i]) for i, (src, dst) in enumerate(pieces)]
    for load in loads[:small]:
        load.start()

    half = pairs // 2
    place = lax.rem(me, half)
    group = me - place
    low_end = place == 0
    high_end = place == half - 1
    up = group + lax.rem(place + 1, half)
    down = group + lax.rem(place + half - 1, half)
    pair_to = [{"pair": up}, {"pair": down}, {"pair": lax.rem(me + half, pairs)}]
    at_edge = [high_end, low_end]
    fit_to = [{"fit": lax.rem(fit + j, fits)} for j in range(1, fits)]
    blk_to = {"blk": 1 - blk}
    barrier = pltpu.get_barrier_semaphore()
    targets = pair_to + fit_to + [blk_to]
    for target in targets:
        pl.semaphore_signal(barrier, inc=1, device_id=target, device_id_type=MESH)

    def rows_of(c, count=1):
        return pl.ds(c * size, count * size)

    def mix_copy(k, c, source=OWN):
        span = rows_of(c)
        return pltpu.make_async_remote_copy(
            src_ref=held.at[source, span],
            dst_ref=held.at[k, span],
            send_sem=mix_send.at[k, c],
            recv_sem=mix_recv.at[k, c],
            device_id=pair_to[k],
            device_id_type=MESH,
        )

    def send_own(c):
        mix_copy(2, c).start()
        for k in range(2):

            @pl.when(jnp.logical_not(at_edge[k]))
            def _():
                mix_copy(k, c).start()

    def forward(c):
        mix_copy(2, c).wait_recv()
        for k in range(2):

            @pl.when(at_edge[k])
            def _():
                mix_copy(k, c, 2).start()

    loads[0].wait()
    loads[1].wait()
    for load in loads[small:]:
        load.start()
    high, low = halves(trans[...])
    trans_high[...] = high
    trans_low[...] = low

    for c in range(CHUNKS):
        span = rows_of(c)
        held[OWN, span, :] = dot3(amp[span, :], trans_high[...], trans_low[...], NT)
        if c == 0:
            pl.semaphore_wait(barrier, len(targets))
        if c < WINDOW:
            send_own(c)

    part_copies = []
    for j in range(fits):
        t = lax.rem(fit + j + 1, fits)
        loads[small + 2 * j].wait()
        high, low = halves(right[t])
        right_high[t] = high
        right_low[t] = low
        loads[small + 1 + 2 * j].wait()
        for c in range(PARTS):
            span = pl.ds(c * part_size, part_size)
            value = dot3(left[t, span, :], right_high[t], right_low[t], NT)
            if j == fits - 1:
                own_part[span, :] = value
                continue
            part_out[j, span, :] = value
            copy = pltpu.make_async_remote_copy(
                src_ref=part_out.at[j, span],
                dst_ref=part_in.at[j, span],
                send_sem=part_send.at[j, c],
                recv_sem=part_recv.at[j, c],
                device_id=fit_to[j],
                device_id_type=MESH,
            )
            copy.start()
            part_copies.append((c, copy))

    for load in loads[2:small]:
        load.wait()
    column = lax.broadcasted_iota(jnp.int32, (rows, width), 1)
    row = lax.broadcasted_iota(jnp.int32, (rows, width), 0) + blk * rows
    vir = vir_ref[...]
    vir_rows = jnp.sum(jnp.where(row == column, vir, 0.0), axis=1, keepdims=True)
    limit = blocks_ref[0] * (width // 4)
    scale = 0.7 / (vir_rows + vir + occ_ref[0])
    inside = (row < limit) & (column < limit)
    gain[...] = jnp.where(inside, scale, 0.0)
    base[...] = jnp.where(inside, 0.3 * amp[...] - scale * own_part[...], 0.0)

    weights = []
    for d in (pairs - 1, 1, half, 0):
        weight = jnp.float32(0.0)
        for k in range(coup_ref.shape[1]):
            shard = neigh_ref[0, k] // fits
            delta = lax.rem(shard - me + pairs, pairs)
            weight = weight + jnp.where(delta == d, coup_ref[0, k], 0.0)
        weights.append(weight)

    def density(f, block, span):
        product = dot3(block, right_high[f], right_low[f], NN)
        return jnp.sum(left[f, span, :] * product, axis=0, keepdims=True)

    def new_copy(j, c):
        span = rows_of(c)
        return pltpu.make_async_remote_copy(
            src_ref=new.at[span],
            dst_ref=new_in.at[j - 1, span],
            send_sem=new_send.at[j - 1, c],
            recv_sem=new_recv.at[j - 1, c],
            device_id=fit_to[j - 1],
            device_id_type=MESH,
        )

    def out_copy(c):
        span = rows_of(c)
        return pltpu.make_async_copy(new.at[span], new_hbm.at[0, span], out_sem.at[c])

    def others(first, count):
        span = rows_of(first, count)
        for j in range(1, fits):
            for c in range(first, first + count):
                new_copy(j, c).wait_recv()
            f = lax.rem(fit + fits - j, fits)
            dens_own[f] += density(f, new_in[j - 1, span, :], span)

    dens_own[...] = jnp.zeros_like(dens_own)
    first = 0
    pending = None
    groups = list(GROUPS)
    for step in range(CHUNKS + AHEAD):
        if step < CHUNKS:
            if step + WINDOW < CHUNKS:
                mix_copy(2, step).wait_send()
                send_own(step + WINDOW)
            forward(step)
        c = step - AHEAD
        if c < 0:
            continue
        span = rows_of(c)
        mix_copy(0, c).wait_recv()
        mix_copy(1, c).wait_recv()
        total = weights[0] * held[0, span, :]
        for k in range(1, 4):
            total = total + weights[k] * held[k, span, :]
        value = dot3(total, trans_high[...], trans_low[...], NN)
        for part, copy in part_copies:
            if c % (CHUNKS // PARTS) == 0 and part == c // (CHUNKS // PARTS):
                copy.wait_recv()
        for j in range(fits - 1):
            value = value - part_in[j, span, :]
        new[span, :] = base[span, :] + gain[span, :] * value
        for j in range(1, fits):
            new_copy(j, c).start()
        out_copy(c).start()
        if pending is not None:
            others(*pending)
            pending = None
        if c + 1 == first + groups[0]:
            span = rows_of(first, groups[0])
            dens_own[fit] += density(fit, new[span, :], span)
            pending = (first, groups.pop(0))
            first = c + 1
    others(*pending)

    copy = pltpu.make_async_remote_copy(
        src_ref=dens_own, dst_ref=dens_in, send_sem=dens_send, recv_sem=dens_recv,
        device_id=blk_to, device_id_type=MESH,
    )
    copy.start()
    for c in range(CHUNKS):
        for k in range(2):
            mix_copy(k, c).wait_send()
        if c + WINDOW >= CHUNKS:
            mix_copy(2, c).wait_send()
        for j in range(1, fits):
            new_copy(j, c).wait_send()
        out_copy(c).wait()
    for _, part in part_copies:
        part.wait_send()
    copy.wait()
    for f in range(fits):
        dens_ref[f : f + 1, :] = dens_own[f] + dens_in[f]


def deliver(new_hbm, dens_hbm, new_out, dens_out, new, dens, in_sem, out_sem):
    reads = [
        pltpu.make_async_copy(new_hbm, new, in_sem.at[0]),
        pltpu.make_async_copy(dens_hbm, dens, in_sem.at[1]),
    ]
    writes = [
        pltpu.make_async_copy(new, new_out, out_sem.at[0]),
        pltpu.make_async_copy(dens, dens_out, out_sem.at[1]),
    ]
    for read in reads:
        read.start()
    for read, write in zip(reads, writes):
        read.wait()
        write.start()
    for write in writes:
        write.wait()


def body(fits, pairs, left, right, amp, trans, vir, occ, coup, neigh, blocks):
    rows, width = amp.shape[1:]
    aux = left.shape[2]
    hbm = pl.BlockSpec(memory_space=pltpu.HBM)
    vmem = pl.BlockSpec(memory_space=pltpu.VMEM)
    dma = pltpu.SemaphoreType.DMA
    plane = pltpu.VMEM((rows, width), F32)
    square = pltpu.VMEM((width, width), BF16)
    partner = pltpu.VMEM((fits - 1, rows, width), F32)
    flops = 2 * 3 * 2 * (fits * rows * width * aux + rows * width * width)
    results = pl.pallas_call(
        functools.partial(kernel, fits, pairs),
        out_shape=(
            jax.ShapeDtypeStruct(amp.shape, F32),
            jax.ShapeDtypeStruct((fits, aux), F32),
        ),
        in_specs=[hbm] * 9,
        out_specs=(pl.BlockSpec(memory_space=pl.ANY), vmem),
        scratch_shapes=[
            pltpu.VMEM((fits, rows, aux), F32),
            pltpu.VMEM((fits, width, aux), F32),
            plane,
            pltpu.VMEM((width, width), F32),
            pltpu.VMEM(vir.shape, F32),
            pltpu.SMEM(occ.shape, F32),
            pltpu.SMEM(coup.shape, F32),
            pltpu.SMEM(neigh.shape, jnp.int32),
            pltpu.SMEM(blocks.shape, jnp.int32),
            square,
            square,
            pltpu.VMEM((fits, width, aux), BF16),
            pltpu.VMEM((fits, width, aux), BF16),
            pltpu.VMEM((4, rows, width), F32),
            partner,
            partner,
            plane,
            plane,
            plane,
            plane,
            partner,
            pltpu.VMEM((fits, 1, aux), F32),
            pltpu.VMEM((fits, 1, aux), F32),
            dma((7 + 2 * fits,)),
            dma((3, CHUNKS)),
            dma((3, CHUNKS)),
            dma((fits - 1, PARTS)),
            dma((fits - 1, PARTS)),
            dma((fits - 1, CHUNKS)),
            dma((fits - 1, CHUNKS)),
            dma,
            dma,
            dma((CHUNKS,)),
        ],
        compiler_params=pltpu.CompilerParams(
            collective_id=0, has_side_effects=True, vmem_limit_bytes=64 * 2**20
        ),
        cost_estimate=pl.CostEstimate(flops=flops, bytes_accessed=2**23, transcendentals=0),
    )(left, right, amp, trans, vir, occ, coup, neigh, blocks)
    return pl.pallas_call(
        deliver,
        out_shape=tuple(jax.ShapeDtypeStruct(r.shape, F32) for r in results),
        in_specs=[hbm] * 2,
        out_specs=(hbm, hbm),
        scratch_shapes=[pltpu.VMEM(r.shape, F32) for r in results] + [dma((2,)), dma((2,))],
        cost_estimate=pl.CostEstimate(flops=0, bytes_accessed=2**20, transcendentals=0),
    )(*results)


def solution(mesh):
    placed = (
        P("pair", "blk", "fit"),
        P("pair", None, "fit"),
        P(("pair", "fit"), "blk", None),
        P(("pair", "fit"), None, None),
        P(("pair", "fit"), None),
        P(("pair", "fit")),
        P(("pair", "fit"), None),
        P(("pair", "fit"), None),
        P(("pair", "fit")),
    )
    return jax.shard_map(
        functools.partial(body, mesh.shape["fit"], mesh.shape["pair"]),
        mesh=mesh,
        in_specs=placed,
        out_specs=(P(("pair", "fit"), "blk", None), P("pair", "fit")),
        check_vma=False,
    )
```
